256 devices in a mesh: row: 16 (over z, core), col: 16 (over x, y).
Axes of the slice: x: 4, y: 4, z: 8, core: 2. Of those that a mesh axis runs over, the one named last changes fastest.
Arguments:
- tokens: bfloat16 [1024, 6144], P('col', 'row'), may hold values from -6 to 6
- w_in: bfloat16 [6144, 24576], P('row', 'col'), may hold values from -0.078125 to 0.078125
- w_out: bfloat16 [24576, 6144], P('col', 'row'), may hold values from -0.0390625 to 0.0390625
- d_output: bfloat16 [1024, 6144], P('col', 'row'), may hold values from -6 to 6
Outputs:
- output: float32 [1024, 6144], P('col', 'row')
- grad_tokens: float32 [1024, 6144], P('col', 'row')
- grad_w_in: float32 [6144, 24576], P('row', 'col')
- grad_w_out: float32 [24576, 6144], P('col', 'row')
The draws below stay inside these ranges and needn't reach their ends.
All inputs are finite; a program needn't handle non-finite values.
Results may differ from the reference program's by a relative error of at most 0.0029.
Values may be sent and summed in bfloat16 or wider, within the bound.
A program may use at most 128 MiB of HBM per device.

```python
import jax
import jax.numpy as jnp
from jax import lax

D = 6144
FF = 24576
TOKENS = 1024


def level_of(own_key, dims, pieces, smallest, top_value):
    gain = 1.0
    for dim, parts in pieces:
        heights = jax.random.uniform(jax.random.fold_in(jax.random.fold_in(own_key, 6), dim), (parts,), jnp.float32, smallest / len(pieces), top_value / len(pieces))
        gain = gain * jnp.repeat(jnp.exp(heights), dims[dim] // parts).reshape((-1,) + (1,) * (len(dims) - 1 - dim))
    return gain


def gaussian(key, extent, spread, reach, split=(), kind=jnp.bfloat16):
    array = spread * jax.random.normal(key, extent, jnp.float32)
    if split:
        array = array * level_of(key, extent, split, -0.22, 0.18)
    return jnp.clip(array, -reach, reach).astype(kind)


def setup_inputs(seed: int = 0) -> dict:
    seeds = jax.random.split(jax.random.key(seed), 5)
    tokens = gaussian(seeds[0], (TOKENS, D), 1.0, 6.0, ((0, 16), (1, 16)))
    w_in = gaussian(seeds[1], (D, FF), D ** -0.5, 0.078125, ((0, 16), (1, 16)))
    w_out = gaussian(seeds[2], (FF, D), FF ** -0.5, 0.0390625, ((0, 16), (1, 16)))
    d_output = gaussian(seeds[3], (TOKENS, D), 1.0, 6.0, ((0, 16), (1, 16)))
    return {"tokens": tokens, "w_in": w_in, "w_out": w_out, "d_output": d_output}


def gelu_exact(values):
    return values * 0.5 * (1.0 + lax.erf(values * 0.7071067811865476))


def gelu_slope(values):
    normal_cdf = 0.5 * (1.0 + lax.erf(values * 0.7071067811865476))
    return normal_cdf + values * jnp.exp(-0.5 * values * values) * 0.3989422804014327


def reference(tokens, w_in, w_out, d_output):
    hidden = jnp.dot(tokens, w_in, preferred_element_type=jnp.float32)
    activation = gelu_exact(hidden).astype(jnp.bfloat16)
    output = jnp.dot(activation, w_out, preferred_element_type=jnp.float32)
    grad_w_out = jnp.dot(activation.T, d_output, preferred_element_type=jnp.float32)
    grad_activation = jnp.dot(d_output, w_out.T, preferred_element_type=jnp.float32)
    grad_hidden = (grad_activation * gelu_slope(hidden)).astype(jnp.bfloat16)
    grad_w_in = jnp.dot(tokens.T, grad_hidden, preferred_element_type=jnp.float32)
    grad_tokens = jnp.dot(grad_hidden, w_in.T, preferred_element_type=jnp.float32)
    return output, grad_tokens, grad_w_in, grad_w_out
```

```python
import functools

import jax
import jax.numpy as jnp
from jax import lax
from jax.experimental import pallas as pl
from jax.experimental.pallas import tpu as pltpu
from jax.sharding import PartitionSpec as P

F32, BF16 = jnp.float32, jnp.bfloat16
MESH = pl.DeviceIdType.MESH
NZ = 8
BLK = 64
WID = 384
HID = 1536
HALF = 768
NCH = 4
CHR = 256
RZ = CHR // NZ
SUM_SCALE = 2.0**19
OUT_SCALE = 2.0**9

OFFS = [
    (0, 0), (0, 1), (0, 3), (0, 2),
    (2, 2), (2, 1), (2, 3), (1, 2),
    (3, 2), (3, 1), (3, 3), (1, 3),
    (1, 1), (2, 0), (3, 0), (1, 0),
]


def gelu_exact(values):
    return values * 0.5 * (1.0 + lax.erf(values * 0.7071067811865476))


def gelu_slope(values):
    normal_cdf = 0.5 * (1.0 + lax.erf(values * 0.7071067811865476))
    return normal_cdf + values * jnp.exp(-0.5 * values * values) * 0.3989422804014327


def enc(v):
    return ((v * jnp.abs(v)) * (v * v)).astype(BF16)


def dec(code):
    y = code.astype(F32)
    root = lax.rsqrt(lax.rsqrt(jnp.abs(y)))
    return jnp.where(y == 0.0, 0.0, jnp.where(y < 0.0, -root, root))


def kernel(
    tok_ref, win_ref, wout_ref, dout_ref,
    out_ref, gt_ref, gwi_ref, gwo_ref,
    acts, xs, wc0, wc1, part, snd, rcv, hid, osnd, orcv, osum,
    loc_sem, tok_s, tok_r, fwd_s, fwd_r, w_s, w_r,
    rs_s, rs_r, ag_s, ag_r, sib_s, sib_r, out_s, out_r,
):
    row = lax.axis_index("row")
    col = lax.axis_index("col")
    z, core = row // 2, row % 2
    x, y = col // 4, col % 4
    other = 1 - core
    sib = (z * 2 + other, col)
    z_to = [(((z + 1) % NZ) * 2 + core, col), (((z + NZ - 1) % NZ) * 2 + core, col)]

    def shift(by):
        return (z + by + NZ) % NZ

    def peer(dx, dy):
        return (row, ((x + dx + 4) % 4) * 4 + (y + dy + 4) % 4)

    own_w = pl.ds(pl.multiple_of(core * WID, WID), WID)
    own_h = pl.ds(pl.multiple_of(core * HALF, HALF), HALF)
    oth_h = pl.ds(pl.multiple_of(other * HALF, HALF), HALF)
    halves = [pl.ds(0, WID), pl.ds(WID, WID)]
    x_in = [tok_ref, dout_ref]

    def remote(src, dst, s, r, dev):
        return pltpu.make_async_remote_copy(
            src_ref=src, dst_ref=dst, send_sem=s, recv_sem=r, device_id=dev, device_id_type=MESH
        )

    barrier = pltpu.get_barrier_semaphore()
    greeted = [sib, *z_to] + [peer(dx, dy) for dx, dy in OFFS[1:]]
    for dev in greeted:
        pl.semaphore_signal(barrier, inc=1, device_id=dev, device_id_type=MESH)
    local = [
        pltpu.make_async_copy(tok_ref, xs.at[0, pl.ds(0, BLK), own_w], loc_sem.at[0]),
        pltpu.make_async_copy(dout_ref, xs.at[1, pl.ds(0, BLK), own_w], loc_sem.at[1]),
        pltpu.make_async_copy(win_ref.at[:, own_h], wc0.at[own_w, :], loc_sem.at[2]),
        pltpu.make_async_copy(wout_ref.at[own_h, :], wc1.at[:, own_w], loc_sem.at[3]),
    ]
    for c in local:
        c.start()
    pl.semaphore_wait(barrier, len(greeted))

    def tok_copy(t, p):
        dx, dy = OFFS[p]
        return remote(
            x_in[t], xs.at[t, pl.ds(p * BLK, BLK), own_w], tok_s.at[t, p], tok_r.at[t, p], peer(-dx, -dy)
        )

    def fwd_copy(t, k):
        place = xs.at[t, pl.ds(k * CHR, CHR), own_w]
        return remote(place, place, fwd_s.at[t, k], fwd_r.at[t, k], sib)

    w_copies = [
        remote(win_ref.at[:, oth_h], wc0.at[own_w, :], w_s.at[0], w_r.at[0], sib),
        remote(wout_ref.at[oth_h, :], wc1.at[:, own_w], w_s.at[1], w_r.at[1], sib),
    ]

    for t in range(2):
        for p in range(1, 4):
            tok_copy(t, p).start()
        w_copies[t].start()
    for c in local:
        c.wait()
    for p in range(4, 16):
        for t in range(2):
            tok_copy(t, p).start()

    def arrive(t, k):
        for p in range(4 * k, 4 * k + 4):
            if p:
                tok_copy(t, p).wait_recv()
        fwd_copy(t, k).start()

    def partial(t, k):
        fwd_copy(t, k).wait_recv()
        rows = pl.ds(k * CHR, CHR)

        def tile(n, carry):
            cols = pl.ds(pl.multiple_of(n * 256, 256), 256)
            if t == 0:
                got = jnp.dot(xs[0, rows, :], wc0[:, cols], preferred_element_type=F32)
            else:
                got = lax.dot_general(
                    xs[1, rows, :], wc1[cols, :], (((1,), (1,)), ((), ())), preferred_element_type=F32
                )
            part[t, k, :, cols] = got * SUM_SCALE
            return carry

        lax.fori_loop(0, HALF // 256, tile, 0)

    def rs_copy(t, k, d, r):
        at = (t, k, d, r)
        if r == 0:
            src, dst = snd.at[t, k, d, r, :, halves[d]], rcv.at[t, k, d, r, :, halves[d]]
        else:
            src, dst = snd.at[at], rcv.at[at]
        return remote(src, dst, rs_s.at[at], rs_r.at[at], z_to[d])

    def rs_one(t, k, r):
        for d in range(2):
            owner = shift(4 - r if d == 0 else r - 4)
            rows = pl.ds(pl.multiple_of(owner * RZ, RZ), RZ)
            mine = halves[d]
            if r == 0:
                snd[t, k, d, r, :, mine] = enc(part[t, k, rows, mine])
            else:
                rs_copy(t, k, d, r - 1).wait_recv()
                if r == 1:
                    rest = halves[1 - d]
                    snd[t, k, d, r, :, mine] = enc(dec(rcv[t, k, d, 0, :, mine]) + part[t, k, rows, mine])
                    snd[t, k, d, r, :, rest] = enc(part[t, k, rows, rest])
                else:
                    snd[t, k, d, r] = enc(dec(rcv[t, k, d, r - 1]) + part[t, k, rows, :])
            rs_copy(t, k, d, r).start()

    def both(fn):
        def body(t, carry):
            fn(t)
            return carry

        lax.fori_loop(0, 2, body, 0)

    def rs(k, r):
        both(lambda t: rs_one(t, k, r))

    def ag_copy(t, k, d, r, b):
        rows = pl.ds(pl.multiple_of(k * CHR + b * RZ, RZ), RZ)
        if r == 3:
            cols = pl.ds(pl.multiple_of(core * HALF + d * WID, WID), WID)
        else:
            cols = own_h
        place = acts.at[t, rows, cols]
        return remote(place, place, ag_s.at[t, k, d, r], ag_r.at[t, k, d, r], z_to[d])

    def ag_wait(t, k, d, r):
        ag_copy(t, k, d, r, shift(-(r + 1) if d == 0 else r + 1)).wait_recv()

    def ag_one(t, k, r):
        for d in range(2):
            if r:
                ag_wait(t, k, d, r - 1)
            ag_copy(t, k, d, r, shift(-r if d == 0 else r)).start()

    def ag(k, r):
        both(lambda t: ag_one(t, k, r))

    def settle(k):
        rows = pl.ds(pl.multiple_of(z * RZ, RZ), RZ)
        place = pl.ds(pl.multiple_of(k * CHR + z * RZ, RZ), RZ)
        for t in range(2):
            for d in range(2):
                rs_copy(t, k, d, 3).wait_recv()
            total = (dec(rcv[t, k, 0, 3]) + dec(rcv[t, k, 1, 3]) + part[t, k, rows, :]) * (1.0 / SUM_SCALE)
            if t == 0:
                hid[...] = total
                acts[0, place, own_h] = gelu_exact(total).astype(BF16)
            else:
                acts[1, place, own_h] = (total * gelu_slope(hid[...])).astype(BF16)
            ag_one(t, k, 0)

    def sib_copy(t, k):
        place = acts.at[t, pl.ds(k * CHR, CHR), own_h]
        return remote(place, place, sib_s.at[t, k], sib_r.at[t, k], sib)

    def gathered(k):
        for t in range(2):
            for d in range(2):
                ag_wait(t, k, d, 3)
            sib_copy(t, k).start()

    def out_copy(t, p):
        return remote(osnd.at[t, p], orcv.at[t, p], out_s.at[t, p], out_r.at[t, p], peer(*OFFS[p]))

    def project(k):
        rows = pl.ds(k * CHR, CHR)
        for t in range(2):
            sib_copy(t, k).wait_recv()
            if t == 0:
                got = jnp.dot(acts[0, rows, :], wout_ref[...], preferred_element_type=F32)
            else:
                got = lax.dot_general(
                    acts[1, rows, :], win_ref[...], (((1,), (1,)), ((), ())), preferred_element_type=F32
                )
            got = got * OUT_SCALE
            for i in range(4):
                p = 4 * k + i
                block = got[i * BLK : (i + 1) * BLK, :]
                if p == 0:
                    osum[t] = block
                else:
                    osnd[t, p] = enc(block)
                    out_copy(t, p).start()

    def weight_grads(k):
        rows = pl.ds(k * CHR, CHR)

        def tile(n, carry):
            cols = pl.ds(pl.multiple_of(n * 256, 256), 256)
            more = lax.dot_general(
                acts[0, rows, cols], xs[1, rows, own_w], (((0,), (0,)), ((), ())), preferred_element_type=F32
            )
            gwo_ref[cols, :] = more if k == 0 else gwo_ref[cols, :] + more
            more = lax.dot_general(
                xs[0, rows, own_w], acts[1, rows, cols], (((0,), (0,)), ((), ())), preferred_element_type=F32
            )
            gwi_ref[:, cols] = more if k == 0 else gwi_ref[:, cols] + more
            return carry

        lax.fori_loop(0, HID // 256, tile, 0)

    arrive(0, 0)
    w_copies[0].wait_recv()
    partial(0, 0)
    rs_one(0, 0, 0)
    arrive(1, 0)
    w_copies[1].wait_recv()
    partial(1, 0)
    rs_one(1, 0, 0)
    for t in range(2):
        arrive(t, 1)
    for t in range(2):
        partial(t, 1)
    rs(0, 1); rs(1, 0)
    for t in range(2):
        arrive(t, 2)
    rs(0, 2); rs(1, 1)
    for t in range(2):
        partial(t, 2)
        arrive(t, 3)
    rs(0, 3); rs(1, 2)
    for t in range(2):
        partial(t, 3)
    settle(0); rs(1, 3); rs(2, 0)
    ag(0, 1); settle(1); rs(2, 1); rs(3, 0)
    ag(0, 2); ag(1, 1); rs(2, 2); rs(3, 1)
    ag(0, 3); ag(1, 2); rs(2, 3); rs(3, 2)
    gathered(0); ag(1, 3); settle(2); rs(3, 3)
    project(0)
    gathered(1); ag(2, 1); settle(3)
    weight_grads(0)
    ag(2, 2); ag(3, 1)
    project(1)
    weight_grads(1)
    ag(2, 3); ag(3, 2)
    gathered(2); ag(3, 3)
    project(2)
    weight_grads(2)
    gathered(3)
    project(3)
    weight_grads(3)

    for t in range(2):
        def add(p, carry, t=t):
            out = remote(osnd.at[t, p], orcv.at[t, p], out_s.at[t, p], out_r.at[t, p], sib)
            out.wait_recv()
            osum[t] = osum[t] + dec(orcv[t, p])
            return carry

        lax.fori_loop(1, 16, add, 0)
    out_ref[...] = osum[0] * (1.0 / OUT_SCALE)
    gt_ref[...] = osum[1] * (1.0 / OUT_SCALE)

    for t in range(2):
        w_copies[t].wait_send()
        for p in range(1, 16):
            tok_copy(t, p).wait_send()
            out_copy(t, p).wait_send()
        for k in range(NCH):
            fwd_copy(t, k).wait_send()
            sib_copy(t, k).wait_send()
            for d in range(2):
                for r in range(4):
                    rs_copy(t, k, d, r).wait_send()
                    ag_copy(t, k, d, r, shift(-r if d == 0 else r)).wait_send()


def shards(tokens, w_in, w_out, d_output):
    vmem = pl.BlockSpec(memory_space=pltpu.VMEM)
    dma = pltpu.SemaphoreType.DMA
    return pl.pallas_call(
        kernel,
        out_shape=(
            jax.ShapeDtypeStruct((BLK, WID), F32),
            jax.ShapeDtypeStruct((BLK, WID), F32),
            jax.ShapeDtypeStruct((WID, HID), F32),
            jax.ShapeDtypeStruct((HID, WID), F32),
        ),
        in_specs=[vmem] * 4,
        out_specs=(vmem,) * 4,
        scratch_shapes=[
            pltpu.VMEM((2, NCH * CHR, HID), BF16),
            pltpu.VMEM((2, NCH * CHR, HALF), BF16),
            pltpu.VMEM((HALF, HALF), BF16),
            pltpu.VMEM((HALF, HALF), BF16),
            pltpu.VMEM((2, NCH, CHR, HALF), F32),
            pltpu.VMEM((2, NCH, 2, 4, RZ, HALF), BF16),
            pltpu.VMEM((2, NCH, 2, 4, RZ, HALF), BF16),
            pltpu.VMEM((RZ, HALF), F32),
            pltpu.VMEM((2, 16, BLK, WID), BF16),
            pltpu.VMEM((2, 16, BLK, WID), BF16),
            pltpu.VMEM((2, BLK, WID), F32),
            dma((4,)),
            dma((2, 16)), dma((2, 16)),
            dma((2, NCH)), dma((2, NCH)),
            dma((2,)), dma((2,)),
            dma((2, NCH, 2, 4)), dma((2, NCH, 2, 4)),
            dma((2, NCH, 2, 4)), dma((2, NCH, 2, 4)),
            dma((2, NCH)), dma((2, NCH)),
            dma((2, 16)), dma((2, 16)),
        ],
        compiler_params=pltpu.CompilerParams(
            collective_id=0, has_side_effects=True, vmem_limit_bytes=56 * 2**20
        ),
    )(tokens, w_in, w_out, d_output)


def solution(mesh):
    placed = (P("col", "row"), P("row", "col"), P("col", "row"), P("col", "row"))
    return jax.shard_map(
        shards,
        mesh=mesh,
        in_specs=placed,
        out_specs=(P("col", "row"), P("col", "row"), P("row", "col"), P("col", "row")),
        check_vma=False,
    )
```

```python
import functools

import jax
import jax.numpy as jnp
from jax import lax
from jax.experimental import pallas as pl
from jax.experimental.pallas import tpu as pltpu
from jax.sharding import PartitionSpec as P

F32, BF16 = jnp.float32, jnp.bfloat16
MESH = pl.DeviceIdType.MESH
NZ = 8
BLK = 64
WID = 384
HID = 1536
HALF = 768
NCH = 4
CHR = 256
RZ = CHR // NZ
SUM_SCALE = 2.0**19
OUT_SCALE = 2.0**9

STEPS = [0, 1, 3, 2]
PART = CHR // 2
SUB = BLK // 2


def gelu_exact(values):
    return values * 0.5 * (1.0 + lax.erf(values * 0.7071067811865476))


def gelu_slope(values):
    normal_cdf = 0.5 * (1.0 + lax.erf(values * 0.7071067811865476))
    return normal_cdf + values * jnp.exp(-0.5 * values * values) * 0.3989422804014327


def enc(v):
    return ((v * jnp.abs(v)) * (v * v)).astype(BF16)


def dec(code):
    y = code.astype(F32)
    root = lax.rsqrt(lax.rsqrt(jnp.abs(y)))
    return jnp.where(y == 0.0, 0.0, jnp.where(y < 0.0, -root, root))


def kernel(
    tok_ref, win_hbm, wout_hbm, dout_ref,
    out_ref, gt_ref, gwi_ref, gwo_ref,
    win_ref, wout_ref, acts, xs, wc0, wc1, part, snd, rcv, hid, osnd, orcv, osum,
    loc_sem, one_s, one_r, two_s, two_r, fwd_s, fwd_r, w_s, w_r,
    rs_s, rs_r, ag_s, ag_r, sib_s, sib_r, last_s, last_r, out_s, out_r,
):
    row = lax.axis_index("row")
    col = lax.axis_index("col")
    z, core = row // 2, row % 2
    x, y = col // 4, col % 4
    other = 1 - core
    sib = (z * 2 + other, col)
    z_to = [(((z + 1) % NZ) * 2 + core, col), (((z + NZ - 1) % NZ) * 2 + core, col)]

    def shift(by):
        return (z + by + NZ) % NZ

    def peer(dx, dy):
        return (row, ((x + dx + 4) % 4) * 4 + (y + dy + 4) % 4)

    own_w = pl.ds(pl.multiple_of(core * WID, WID), WID)
    own_h = pl.ds(pl.multiple_of(core * HALF, HALF), HALF)
    oth_h = pl.ds(pl.multiple_of(other * HALF, HALF), HALF)
    halves = [pl.ds(0, WID), pl.ds(WID, WID)]
    x_in = [tok_ref, dout_ref]

    def remote(src, dst, s, r, dev):
        return pltpu.make_async_remote_copy(
            src_ref=src, dst_ref=dst, send_sem=s, recv_sem=r, device_id=dev, device_id_type=MESH
        )

    barrier = pltpu.get_barrier_semaphore()
    greeted = [sib, *z_to] + [peer(dx, dy) for dx in range(4) for dy in range(4) if dx or dy]
    for dev in greeted:
        pl.semaphore_signal(barrier, inc=1, device_id=dev, device_id_type=MESH)
    local = [
        pltpu.make_async_copy(
            x_in[t].at[pl.ds(ab * SUB, SUB), :], xs.at[t, pl.ds(ab * PART, SUB), own_w], loc_sem.at[t * 2 + ab]
        )
        for t in range(2)
        for ab in range(2)
    ]
    local += [
        pltpu.make_async_copy(win_hbm.at[:, own_h], wc0.at[own_w, :], loc_sem.at[4]),
        pltpu.make_async_copy(wout_hbm.at[own_h, :], wc1.at[:, own_w], loc_sem.at[5]),
        pltpu.make_async_copy(win_hbm, win_ref, loc_sem.at[6]),
        pltpu.make_async_copy(wout_hbm, wout_ref, loc_sem.at[7]),
    ]
    for c in local:
        c.start()
    pl.semaphore_wait(barrier, len(greeted))

    def one_copy(t, ab, i):
        to = peer(0, -STEPS[i]) if ab == 0 else peer(-STEPS[i], 0)
        return remote(
            x_in[t].at[pl.ds(ab * SUB, SUB), :],
            xs.at[t, pl.ds(ab * PART + i * SUB, SUB), own_w],
            one_s.at[t, ab, i], one_r.at[t, ab, i], to,
        )

    def two_copy(t, ab, j):
        to = peer(-STEPS[j], 0) if ab == 0 else peer(0, -STEPS[j])
        return remote(
            xs.at[t, pl.ds(ab * PART, PART), own_w],
            xs.at[t, pl.ds(j * CHR + ab * PART, PART), own_w],
            two_s.at[t, ab, j], two_r.at[t, ab, j], to,
        )

    def fwd_copy(t, k):
        place = xs.at[t, pl.ds(k * CHR, CHR), own_w]
        return remote(place, place, fwd_s.at[t, k], fwd_r.at[t, k], sib)

    w_copies = [
        remote(win_hbm.at[:, oth_h], wc0.at[own_w, :], w_s.at[0], w_r.at[0], sib),
        remote(wout_hbm.at[oth_h, :], wc1.at[:, own_w], w_s.at[1], w_r.at[1], sib),
    ]

    def spread(t, j):
        for ab in range(2):
            two_copy(t, ab, j).start()

    def arrive(t, k):
        for ab in range(2):
            if k:
                two_copy(t, ab, k).wait_recv()
            else:
                local[t * 2 + ab].wait()
                for i in range(1, 4):
                    one_copy(t, ab, i).wait_recv()
        fwd_copy(t, k).start()

    def partial(t, k):
        fwd_copy(t, k).wait_recv()
        rows = pl.ds(k * CHR, CHR)

        def tile(n, carry):
            cols = pl.ds(pl.multiple_of(n * 256, 256), 256)
            if t == 0:
                got = jnp.dot(xs[0, rows, :], wc0[:, cols], preferred_element_type=F32)
            else:
                got = lax.dot_general(
                    xs[1, rows, :], wc1[cols, :], (((1,), (1,)), ((), ())), preferred_element_type=F32
                )
            part[t, k, :, cols] = got * SUM_SCALE
            return carry

        lax.fori_loop(0, HALF // 256, tile, 0)

    def rs_copy(t, k, d, r):
        at = (t, k, d, r)
        if r == 0:
            src, dst = snd.at[t, k, d, r, :, halves[d]], rcv.at[t, k, d, r, :, halves[d]]
        else:
            src, dst = snd.at[at], rcv.at[at]
        return remote(src, dst, rs_s.at[at], rs_r.at[at], z_to[d])

    def rs_one(t, k, r):
        for d in range(2):
            owner = shift(4 - r if d == 0 else r - 4)
            rows = pl.ds(pl.multiple_of(owner * RZ, RZ), RZ)
            mine = halves[d]
            if r == 0:
                snd[t, k, d, r, :, mine] = enc(part[t, k, rows, mine])
            else:
                rs_copy(t, k, d, r - 1).wait_recv()
                if r == 1:
                    rest = halves[1 - d]
                    snd[t, k, d, r, :, mine] = enc(dec(rcv[t, k, d, 0, :, mine]) + part[t, k, rows, mine])
                    snd[t, k, d, r, :, rest] = enc(part[t, k, rows, rest])
                else:
                    snd[t, k, d, r] = enc(dec(rcv[t, k, d, r - 1]) + part[t, k, rows, :])
            rs_copy(t, k, d, r).start()

    def both(fn):
        def body(t, carry):
            fn(t)
            return carry

        lax.fori_loop(0, 2, body, 0)

    def rs(k, r):
        both(lambda t: rs_one(t, k, r))

    def ag_copy(t, k, d, r, b):
        rows = pl.ds(pl.multiple_of(k * CHR + b * RZ, RZ), RZ)
        if r == 3:
            cols = pl.ds(pl.multiple_of(core * HALF + d * WID, WID), WID)
        else:
            cols = own_h
        place = acts.at[t, rows, cols]
        return remote(place, place, ag_s.at[t, k, d, r], ag_r.at[t, k, d, r], z_to[d])

    def ag_wait(t, k, d, r):
        ag_copy(t, k, d, r, shift(-(r + 1) if d == 0 else r + 1)).wait_recv()

    def ag_one(t, k, r):
        for d in range(2):
            if r:
                ag_wait(t, k, d, r - 1)
            block = shift(-r if d == 0 else r)
            ag_copy(t, k, d, r, block).start()
            if k == NCH - 1 and (r or d == 0):
                last_copy(t, d * 3 + r, block).start()

    def ag(k, r):
        both(lambda t: ag_one(t, k, r))

    def settle(k):
        rows = pl.ds(pl.multiple_of(z * RZ, RZ), RZ)
        place = pl.ds(pl.multiple_of(k * CHR + z * RZ, RZ), RZ)
        for t in range(2):
            for d in range(2):
                rs_copy(t, k, d, 3).wait_recv()
            total = (dec(rcv[t, k, 0, 3]) + dec(rcv[t, k, 1, 3]) + part[t, k, rows, :]) * (1.0 / SUM_SCALE)
            if t == 0:
                hid[...] = total
                acts[0, place, own_h] = gelu_exact(total).astype(BF16)
            else:
                acts[1, place, own_h] = (total * gelu_slope(hid[...])).astype(BF16)
            ag_one(t, k, 0)

    def sib_copy(t, k):
        place = acts.at[t, pl.ds(k * CHR, CHR), own_h]
        return remote(place, place, sib_s.at[t, k], sib_r.at[t, k], sib)

    def last_copy(t, i, block):
        rows = pl.ds(pl.multiple_of((NCH - 1) * CHR + block * RZ, RZ), RZ)
        place = acts.at[t, rows, own_h]
        return remote(place, place, last_s.at[t, i], last_r.at[t, i], sib)

    def last_block(i):
        return shift(-i if i < 4 else i - 3) if i < 7 else shift(4)

    def gathered(k):
        for t in range(2):
            for d in range(2):
                ag_wait(t, k, d, 3)
            if k == NCH - 1:
                last_copy(t, 7, shift(4)).start()
            else:
                sib_copy(t, k).start()

    def out_copy(t, ab, n):
        near, far = STEPS[n // 4], STEPS[n % 4]
        to = peer(near, far) if ab == 0 else peer(far, near)
        return remote(osnd.at[t, ab, n], orcv.at[t, ab, n], out_s.at[t, ab, n], out_r.at[t, ab, n], to)

    def project(k):
        rows = pl.ds(k * CHR, CHR)
        for t in range(2):
            if k == NCH - 1:
                for i in range(8):
                    last_copy(t, i, last_block(i)).wait_recv()
            else:
                sib_copy(t, k).wait_recv()
            if t == 0:
                got = jnp.dot(acts[0, rows, :], wout_ref[...], preferred_element_type=F32)
            else:
                got = lax.dot_general(
                    acts[1, rows, :], win_ref[...], (((1,), (1,)), ((), ())), preferred_element_type=F32
                )
            got = got * OUT_SCALE
            for ab in range(2):
                for i in range(4):
                    n = 4 * k + i
                    block = got[ab * PART + i * SUB : ab * PART + (i + 1) * SUB, :]
                    if n == 0:
                        osum[t, pl.ds(ab * SUB, SUB), :] = block
                    else:
                        osnd[t, ab, n] = enc(block)
                        out_copy(t, ab, n).start()

    def weight_grads(k):
        rows = pl.ds(k * CHR, CHR)

        def tile(n, carry):
            cols = pl.ds(pl.multiple_of(n * 256, 256), 256)
            more = lax.dot_general(
                acts[0, rows, cols], xs[1, rows, own_w], (((0,), (0,)), ((), ())), preferred_element_type=F32
            )
            gwo_ref[cols, :] = more if k == 0 else gwo_ref[cols, :] + more
            more = lax.dot_general(
                xs[0, rows, own_w], acts[1, rows, cols], (((0,), (0,)), ((), ())), preferred_element_type=F32
            )
            gwi_ref[:, cols] = more if k == 0 else gwi_ref[:, cols] + more
            return carry

        lax.fori_loop(0, HID // 256, tile, 0)

    for t in range(2):
        for i in range(1, 4):
            for ab in range(2):
                one_copy(t, ab, i).start()
        w_copies[t].start()
    for t in range(2):
        arrive(t, 0)
        spread(t, 1)
    for t in range(2):
        local[4 + t].wait()
        w_copies[t].wait_recv()
        partial(t, 0)
        rs_one(t, 0, 0)
    for j in range(2, NCH):
        for t in range(2):
            spread(t, j)
    for t in range(2):
        arrive(t, 1)
    for t in range(2):
        partial(t, 1)
    rs(0, 1); rs(1, 0)
    for t in range(2):
        arrive(t, 2)
    rs(0, 2); rs(1, 1)
    for t in range(2):
        partial(t, 2)
    rs(0, 3); rs(1, 2); rs(2, 0)
    for t in range(2):
        arrive(t, 3)
    settle(0); rs(1, 3); rs(2, 1)
    for t in range(2):
        partial(t, 3)
    ag(0, 1); settle(1); rs(2, 2); rs(3, 0)
    ag(0, 2); ag(1, 1); rs(2, 3); rs(3, 1)
    ag(0, 3); ag(1, 2); settle(2); rs(3, 2)
    gathered(0); ag(1, 3); ag(2, 1); rs(3, 3)
    gathered(1); ag(2, 2); settle(3)
    for t in range(2):
        local[6 + t].wait()
    project(0)
    ag(2, 3); ag(3, 1)
    project(1)
    weight_grads(0)
    gathered(2); ag(3, 2)
    weight_grads(1)
    ag(3, 3)
    project(2)
    weight_grads(2)
    gathered(3)
    project(3)
    weight_grads(3)
    for t in range(2):
        for ab in range(2):
            rows = pl.ds(ab * SUB, SUB)

            def add(n, carry, t=t, ab=ab, rows=rows):
                remote(
                    osnd.at[t, ab, n], orcv.at[t, ab, n], out_s.at[t, ab, n], out_r.at[t, ab, n], sib
                ).wait_recv()
                osum[t, rows, :] = osum[t, rows, :] + dec(orcv[t, ab, n])
                return carry

            lax.fori_loop(1, 16, add, 0)
    out_ref[...] = osum[0] * (1.0 / OUT_SCALE)
    gt_ref[...] = osum[1] * (1.0 / OUT_SCALE)

    for t in range(2):
        w_copies[t].wait_send()
        for ab in range(2):
            for i in range(1, 4):
                one_copy(t, ab, i).wait_send()
                two_copy(t, ab, i).wait_send()
            for n in range(1, 16):
                out_copy(t, ab, n).wait_send()
        for i in range(8):
            last_copy(t, i, last_block(i)).wait_send()
        for k in range(NCH):
            fwd_copy(t, k).wait_send()
            if k < NCH - 1:
                sib_copy(t, k).wait_send()
            for d in range(2):
                for r in range(4):
                    rs_copy(t, k, d, r).wait_send()
                    ag_copy(t, k, d, r, shift(-r if d == 0 else r)).wait_send()


def shards(tokens, w_in, w_out, d_output):
    vmem = pl.BlockSpec(memory_space=pltpu.VMEM)
    dma = pltpu.SemaphoreType.DMA
    return pl.pallas_call(
        kernel,
        out_shape=(
            pltpu.VMEM((BLK, WID), F32),
            pltpu.VMEM((BLK, WID), F32),
            pltpu.VMEM((WID, HID), F32),
            pltpu.VMEM((HID, WID), F32),
        ),
        in_specs=[pl.BlockSpec(memory_space=pl.ANY)] * 4,
        out_specs=(vmem,) * 4,
        scratch_shapes=[
            pltpu.VMEM((WID, HID), BF16),
            pltpu.VMEM((HID, WID), BF16),
            pltpu.VMEM((2, NCH * CHR, HID), BF16),
            pltpu.VMEM((2, NCH * CHR, HALF), BF16),
            pltpu.VMEM((HALF, HALF), BF16),
            pltpu.VMEM((HALF, HALF), BF16),
            pltpu.VMEM((2, NCH, CHR, HALF), F32),
            pltpu.VMEM((2, NCH, 2, 4, RZ, HALF), BF16),
            pltpu.VMEM((2, NCH, 2, 4, RZ, HALF), BF16),
            pltpu.VMEM((RZ, HALF), F32),
            pltpu.VMEM((2, 2, 16, SUB, WID), BF16),
            pltpu.VMEM((2, 2, 16, SUB, WID), BF16),
            pltpu.VMEM((2, BLK, WID), F32),
            dma((8,)),
            dma((2, 2, 4)), dma((2, 2, 4)),
            dma((2, 2, 4)), dma((2, 2, 4)),
            dma((2, NCH)), dma((2, NCH)),
            dma((2,)), dma((2,)),
            dma((2, NCH, 2, 4)), dma((2, NCH, 2, 4)),
            dma((2, NCH, 2, 4)), dma((2, NCH, 2, 4)),
            dma((2, NCH)), dma((2, NCH)),
            dma((2, 8)), dma((2, 8)),
            dma((2, 2, 16)), dma((2, 2, 16)),
        ],
        compiler_params=pltpu.CompilerParams(
            collective_id=0, has_side_effects=True, vmem_limit_bytes=56 * 2**20
        ),
    )(tokens, w_in, w_out, d_output)


def solution(mesh):
    placed = (P("col", "row"), P("row", "col"), P("col", "row"), P("col", "row"))
    return jax.shard_map(
        shards,
        mesh=mesh,
        in_specs=placed,
        out_specs=(P("col", "row"), P("col", "row"), P("row", "col"), P("col", "row")),
        check_vma=False,
    )
```

```python
import functools

import jax
import jax.numpy as jnp
from jax import lax
from jax.experimental import pallas as pl
from jax.experimental.pallas import tpu as pltpu
from jax.sharding import PartitionSpec as P

F32, BF16 = jnp.float32, jnp.bfloat16
MESH = pl.DeviceIdType.MESH
NZ = 8
BLK = 64
WID = 384
HID = 1536
HALF = 768
NCH = 4
CHR = 256
RZ = CHR // NZ
SUM_SCALE = 2.0**19
OUT_SCALE = 2.0**9

STEPS = [0, 1, 3, 2]
PART = CHR // 2
SUB = BLK // 2
BLOCKWISE = (1, 2, 3)


def gelu_exact(values):
    return values * 0.5 * (1.0 + lax.erf(values * 0.7071067811865476))


def gelu_slope(values):
    normal_cdf = 0.5 * (1.0 + lax.erf(values * 0.7071067811865476))
    return normal_cdf + values * jnp.exp(-0.5 * values * values) * 0.3989422804014327


def enc(v):
    return ((v * jnp.abs(v)) * (v * v)).astype(BF16)


def dec(code):
    y = code.astype(F32)
    root = lax.rsqrt(lax.rsqrt(jnp.abs(y)))
    return jnp.where(y == 0.0, 0.0, jnp.where(y < 0.0, -root, root))


def kernel(
    tok_ref, win_hbm, wout_hbm, dout_ref,
    out_ref, gt_ref, gwi_ref, gwo_ref,
    win_ref, wout_ref, acts, xs, wc0, wc1, part, snd, rcv, hid, osnd, orcv, osum,
    loc_sem, one_s, one_r, two_s, two_r, fwd_s, fwd_r, w_s, w_r,
    rs_s, rs_r, ag_s, ag_r, sib_s, sib_r, blk_s, blk_r, out_s, out_r,
):
    row = lax.axis_index("row")
    col = lax.axis_index("col")
    z, core = row // 2, row % 2
    x, y = col // 4, col % 4
    other = 1 - core
    sib = (z * 2 + other, col)
    z_to = [(((z + 1) % NZ) * 2 + core, col), (((z + NZ - 1) % NZ) * 2 + core, col)]

    def shift(by):
        return (z + by + NZ) % NZ

    def peer(dx, dy):
        return (row, ((x + dx + 4) % 4) * 4 + (y + dy + 4) % 4)

    own_w = pl.ds(pl.multiple_of(core * WID, WID), WID)
    own_h = pl.ds(pl.multiple_of(core * HALF, HALF), HALF)
    oth_h = pl.ds(pl.multiple_of(other * HALF, HALF), HALF)
    halves = [pl.ds(0, WID), pl.ds(WID, WID)]
    x_in = [tok_ref, dout_ref]

    def remote(src, dst, s, r, dev):
        return pltpu.make_async_remote_copy(
            src_ref=src, dst_ref=dst, send_sem=s, recv_sem=r, device_id=dev, device_id_type=MESH
        )

    barrier = pltpu.get_barrier_semaphore()
    greeted = [sib, *z_to] + [peer(dx, dy) for dx in range(4) for dy in range(4) if dx or dy]
    for dev in greeted:
        pl.semaphore_signal(barrier, inc=1, device_id=dev, device_id_type=MESH)
    local = [
        pltpu.make_async_copy(
            x_in[t].at[pl.ds(ab * SUB, SUB), :], xs.at[t, pl.ds(ab * PART, SUB), own_w], loc_sem.at[t * 2 + ab]
        )
        for t in range(2)
        for ab in range(2)
    ]
    local += [
        pltpu.make_async_copy(win_hbm.at[:, own_h], wc0.at[own_w, :], loc_sem.at[4]),
        pltpu.make_async_copy(wout_hbm.at[own_h, :], wc1.at[:, own_w], loc_sem.at[5]),
        pltpu.make_async_copy(win_hbm, win_ref, loc_sem.at[6]),
        pltpu.make_async_copy(wout_hbm, wout_ref, loc_sem.at[7]),
    ]
    for c in local:
        c.start()
    pl.semaphore_wait(barrier, len(greeted))

    def one_copy(t, ab, i):
        to = peer(0, -STEPS[i]) if ab == 0 else peer(-STEPS[i], 0)
        return remote(
            x_in[t].at[pl.ds(ab * SUB, SUB), :],
            xs.at[t, pl.ds(ab * PART + i * SUB, SUB), own_w],
            one_s.at[t, ab, i], one_r.at[t, ab, i], to,
        )

    def two_copy(t, ab, j):
        to = peer(-STEPS[j], 0) if ab == 0 else peer(0, -STEPS[j])
        return remote(
            xs.at[t, pl.ds(ab * PART, PART), own_w],
            xs.at[t, pl.ds(j * CHR + ab * PART, PART), own_w],
            two_s.at[t, ab, j], two_r.at[t, ab, j], to,
        )

    def fwd_copy(t, k):
        place = xs.at[t, pl.ds(k * CHR, CHR), own_w]
        return remote(place, place, fwd_s.at[t, k], fwd_r.at[t, k], sib)

    w_copies = [
        remote(win_hbm.at[:, oth_h], wc0.at[own_w, :], w_s.at[0], w_r.at[0], sib),
        remote(wout_hbm.at[oth_h, :], wc1.at[:, own_w], w_s.at[1], w_r.at[1], sib),
    ]

    def spread(t, j):
        for ab in range(2):
            two_copy(t, ab, j).start()

    def arrive(t, k):
        for ab in range(2):
            if k:
                two_copy(t, ab, k).wait_recv()
            else:
                local[t * 2 + ab].wait()
                for i in range(1, 4):
                    one_copy(t, ab, i).wait_recv()
        fwd_copy(t, k).start()

    def partial(t, k):
        fwd_copy(t, k).wait_recv()
        rows = pl.ds(k * CHR, CHR)

        if t == 0:
            got = jnp.dot(xs[0, rows, :], wc0[...], preferred_element_type=F32)
        else:
            got = lax.dot_general(xs[1, rows, :], wc1[...], (((1,), (1,)), ((), ())), preferred_element_type=F32)
        part[t, k] = got * SUM_SCALE

    def rs_copy(t, k, d, r):
        at = (t, k, d, r)
        if r == 0:
            src, dst = snd.at[t, k, d, r, :, halves[d]], rcv.at[t, k, d, r, :, halves[d]]
        else:
            src, dst = snd.at[at], rcv.at[at]
        return remote(src, dst, rs_s.at[at], rs_r.at[at], z_to[d])

    def rs_one(t, k, r):
        for d in range(2):
            owner = shift(4 - r if d == 0 else r - 4)
            rows = pl.ds(pl.multiple_of(owner * RZ, RZ), RZ)
            mine = halves[d]
            if r == 0:
                snd[t, k, d, r, :, mine] = enc(part[t, k, rows, mine])
            else:
                rs_copy(t, k, d, r - 1).wait_recv()
                if r == 1:
                    rest = halves[1 - d]
                    snd[t, k, d, r, :, mine] = enc(dec(rcv[t, k, d, 0, :, mine]) + part[t, k, rows, mine])
                    snd[t, k, d, r, :, rest] = enc(part[t, k, rows, rest])
                else:
                    snd[t, k, d, r] = enc(dec(rcv[t, k, d, r - 1]) + part[t, k, rows, :])
            rs_copy(t, k, d, r).start()

    def both(fn):
        def body(t, carry):
            fn(t)
            return carry

        lax.fori_loop(0, 2, body, 0)

    def rs(k, r):
        both(lambda t: rs_one(t, k, r))

    def ag_copy(t, k, d, r, b):
        rows = pl.ds(pl.multiple_of(k * CHR + b * RZ, RZ), RZ)
        if r == 3:
            cols = pl.ds(pl.multiple_of(core * HALF + d * WID, WID), WID)
        else:
            cols = own_h
        place = acts.at[t, rows, cols]
        return remote(place, place, ag_s.at[t, k, d, r], ag_r.at[t, k, d, r], z_to[d])

    def ag_wait(t, k, d, r):
        ag_copy(t, k, d, r, shift(-(r + 1) if d == 0 else r + 1)).wait_recv()

    def ag_one(t, k, r):
        for d in range(2):
            if r:
                ag_wait(t, k, d, r - 1)
            block = shift(-r if d == 0 else r)
            ag_copy(t, k, d, r, block).start()
            if k in BLOCKWISE and (r or d == 0):
                blk_copy(t, k, d * 3 + r, block).start()

    def ag(k, r):
        both(lambda t: ag_one(t, k, r))

    def settle(k):
        rows = pl.ds(pl.multiple_of(z * RZ, RZ), RZ)
        place = pl.ds(pl.multiple_of(k * CHR + z * RZ, RZ), RZ)
        for t in range(2):
            for d in range(2):
                rs_copy(t, k, d, 3).wait_recv()
            total = (dec(rcv[t, k, 0, 3]) + dec(rcv[t, k, 1, 3]) + part[t, k, rows, :]) * (1.0 / SUM_SCALE)
            if t == 0:
                hid[...] = total
                acts[0, place, own_h] = gelu_exact(total).astype(BF16)
            else:
                acts[1, place, own_h] = (total * gelu_slope(hid[...])).astype(BF16)
            ag_one(t, k, 0)

    def sib_copy(t, k):
        place = acts.at[t, pl.ds(k * CHR, CHR), own_h]
        return remote(place, place, sib_s.at[t, k], sib_r.at[t, k], sib)

    def blk_copy(t, k, i, block):
        rows = pl.ds(pl.multiple_of(k * CHR + block * RZ, RZ), RZ)
        place = acts.at[t, rows, own_h]
        at = (t, k - BLOCKWISE[0], i)
        return remote(place, place, blk_s.at[at], blk_r.at[at], sib)

    def block_at(i):
        return shift(-i if i < 4 else i - 3) if i < 7 else shift(4)

    def gathered(k):
        for t in range(2):
            for d in range(2):
                ag_wait(t, k, d, 3)
            if k in BLOCKWISE:
                blk_copy(t, k, 7, shift(4)).start()
            else:
                sib_copy(t, k).start()

    def out_copy(t, ab, n):
        near, far = STEPS[n // 4], STEPS[n % 4]
        to = peer(near, far) if ab == 0 else peer(far, near)
        return remote(osnd.at[t, ab, n], orcv.at[t, ab, n], out_s.at[t, ab, n], out_r.at[t, ab, n], to)

    def project(k):
        rows = pl.ds(k * CHR, CHR)
        for t in range(2):
            if k in BLOCKWISE:
                for i in range(8):
                    blk_copy(t, k, i, block_at(i)).wait_recv()
            else:
                sib_copy(t, k).wait_recv()
            if t == 0:
                got = jnp.dot(acts[0, rows, :], wout_ref[...], preferred_element_type=F32)
            else:
                got = lax.dot_general(
                    acts[1, rows, :], win_ref[...], (((1,), (1,)), ((), ())), preferred_element_type=F32
                )
            got = got * OUT_SCALE
            for ab in range(2):
                for i in range(4):
                    n = 4 * k + i
                    block = got[ab * PART + i * SUB : ab * PART + (i + 1) * SUB, :]
                    if n == 0:
                        osum[t, pl.ds(ab * SUB, SUB), :] = block
                    else:
                        osnd[t, ab, n] = enc(block)
                        out_copy(t, ab, n).start()

    def grad_w_out(k):
        rows = pl.ds(k * CHR, 2 * CHR)

        def tile(n, carry):
            cols = pl.ds(pl.multiple_of(n * 256, 256), 256)
            more = lax.dot_general(
                acts[0, rows, cols], xs[1, rows, own_w], (((0,), (0,)), ((), ())), preferred_element_type=F32
            )
            gwo_ref[cols, :] = more if k == 0 else gwo_ref[cols, :] + more
            return carry

        lax.fori_loop(0, HID // 256, tile, 0)

    def grad_w_in(k):
        rows = pl.ds(k * CHR, 2 * CHR)

        def tile(n, carry):
            cols = pl.ds(pl.multiple_of(n * 256, 256), 256)
            more = lax.dot_general(
                xs[0, rows, own_w], acts[1, rows, cols], (((0,), (0,)), ((), ())), preferred_element_type=F32
            )
            gwi_ref[:, cols] = more if k == 0 else gwi_ref[:, cols] + more
            return carry

        lax.fori_loop(0, HID // 256, tile, 0)

    for t in range(2):
        for i in range(1, 4):
            for ab in range(2):
                one_copy(t, ab, i).start()
        w_copies[t].start()
    for t in range(2):
        arrive(t, 0)
        spread(t, 1)
        spread(t, 2)
    for t in range(2):
        local[4 + t].wait()
        w_copies[t].wait_recv()
        partial(t, 0)
        rs_one(t, 0, 0)
    for t in range(2):
        arrive(t, 1)
        arrive(t, 2)
        spread(t, 3)
    rs(0, 1)
    for t in range(2):
        partial(t, 1)
        rs_one(t, 1, 0)
    rs(0, 2)
    for t in range(2):
        partial(t, 2)
        rs_one(t, 2, 0)
    rs(1, 1)
    rs(0, 3); rs(1, 2); rs(2, 1)
    for t in range(2):
        arrive(t, 3)
    settle(0); rs(1, 3); rs(2, 2)
    for t in range(2):
        partial(t, 3)
        rs_one(t, 3, 0)
    ag(0, 1); settle(1); rs(2, 3); rs(3, 1)
    ag(0, 2); ag(1, 1); settle(2); rs(3, 2)
    ag(0, 3); ag(1, 2); ag(2, 1); rs(3, 3)
    for t in range(2):
        local[6 + t].wait()
    gathered(0); ag(1, 3); ag(2, 2); settle(3)
    project(0)
    gathered(1); ag(2, 3); ag(3, 1)
    project(1)
    gathered(2); ag(3, 2)
    project(2)
    ag(3, 3)
    grad_w_out(0)
    gathered(3)
    project(3)
    grad_w_in(0)
    grad_w_out(2)
    grad_w_in(2)
    for t in range(2):
        for ab in range(2):
            rows = pl.ds(ab * SUB, SUB)

            def add(n, carry, t=t, ab=ab, rows=rows):
                remote(
                    osnd.at[t, ab, n], orcv.at[t, ab, n], out_s.at[t, ab, n], out_r.at[t, ab, n], sib
                ).wait_recv()
                osum[t, rows, :] = osum[t, rows, :] + dec(orcv[t, ab, n])
                return carry

            lax.fori_loop(1, 16, add, 0)
    out_ref[...] = osum[0] * (1.0 / OUT_SCALE)
    gt_ref[...] = osum[1] * (1.0 / OUT_SCALE)

    for t in range(2):
        w_copies[t].wait_send()
        for ab in range(2):
            for i in range(1, 4):
                one_copy(t, ab, i).wait_send()
                two_copy(t, ab, i).wait_send()
            for n in range(1, 16):
                out_copy(t, ab, n).wait_send()
        for k in range(NCH):
            fwd_copy(t, k).wait_send()
            if k in BLOCKWISE:
                for i in range(8):
                    blk_copy(t, k, i, block_at(i)).wait_send()
            else:
                sib_copy(t, k).wait_send()
            for d in range(2):
                for r in range(4):
                    rs_copy(t, k, d, r).wait_send()
                    ag_copy(t, k, d, r, shift(-r if d == 0 else r)).wait_send()


def store(out_v, gt_v, gwi_v, gwo_v, out_ref, gt_ref, gwi_ref, gwo_ref, sems):
    pairs = [(gwi_v, gwi_ref), (gwo_v, gwo_ref), (out_v, out_ref), (gt_v, gt_ref)]
    copies = [pltpu.make_async_copy(a, b, sems.at[i]) for i, (a, b) in enumerate(pairs)]
    for c in copies:
        c.start()
    for c in copies:
        c.wait()


def shards(tokens, w_in, w_out, d_output):
    vmem = pl.BlockSpec(memory_space=pltpu.VMEM)
    dma = pltpu.SemaphoreType.DMA
    shapes = [(BLK, WID), (BLK, WID), (WID, HID), (HID, WID)]
    results = pl.pallas_call(
        kernel,
        out_shape=tuple(pltpu.VMEM(shape, F32) for shape in shapes),
        in_specs=[pl.BlockSpec(memory_space=pl.ANY)] * 4,
        out_specs=(vmem,) * 4,
        scratch_shapes=[
            pltpu.VMEM((WID, HID), BF16),
            pltpu.VMEM((HID, WID), BF16),
            pltpu.VMEM((2, NCH * CHR, HID), BF16),
            pltpu.VMEM((2, NCH * CHR, HALF), BF16),
            pltpu.VMEM((HALF, HALF), BF16),
            pltpu.VMEM((HALF, HALF), BF16),
            pltpu.VMEM((2, NCH, CHR, HALF), F32),
            pltpu.VMEM((2, NCH, 2, 4, RZ, HALF), BF16),
            pltpu.VMEM((2, NCH, 2, 4, RZ, HALF), BF16),
            pltpu.VMEM((RZ, HALF), F32),
            pltpu.VMEM((2, 2, 16, SUB, WID), BF16),
            pltpu.VMEM((2, 2, 16, SUB, WID), BF16),
            pltpu.VMEM((2, BLK, WID), F32),
            dma((8,)),
            dma((2, 2, 4)), dma((2, 2, 4)),
            dma((2, 2, 4)), dma((2, 2, 4)),
            dma((2, NCH)), dma((2, NCH)),
            dma((2,)), dma((2,)),
            dma((2, NCH, 2, 4)), dma((2, NCH, 2, 4)),
            dma((2, NCH, 2, 4)), dma((2, NCH, 2, 4)),
            dma((2, NCH)), dma((2, NCH)),
            dma((2, 3, 8)), dma((2, 3, 8)),
            dma((2, 2, 16)), dma((2, 2, 16)),
        ],
        compiler_params=pltpu.CompilerParams(
            collective_id=0, has_side_effects=True, vmem_limit_bytes=56 * 2**20
        ),
    )(tokens, w_in, w_out, d_output)
    return pl.pallas_call(
        store,
        out_shape=tuple(jax.ShapeDtypeStruct(shape, F32) for shape in shapes),
        in_specs=[pl.BlockSpec(memory_space=pl.ANY)] * 4,
        out_specs=(pl.BlockSpec(memory_space=pl.ANY),) * 4,
        scratch_shapes=[dma((4,))],
        compiler_params=pltpu.CompilerParams(vmem_limit_bytes=2**20),
    )(*results)


def solution(mesh):
    placed = (P("col", "row"), P("row", "col"), P("col", "row"), P("col", "row"))
    return jax.shard_map(
        shards,
        mesh=mesh,
        in_specs=placed,
        out_specs=(P("col", "row"), P("col", "row"), P("row", "col"), P("col", "row")),
        check_vma=False,
    )
```

```python
import functools

import jax
import jax.numpy as jnp
from jax import lax
from jax.experimental import pallas as pl
from jax.experimental.pallas import tpu as pltpu
from jax.sharding import PartitionSpec as P

F32, BF16 = jnp.float32, jnp.bfloat16
MESH = pl.DeviceIdType.MESH
NZ = 8
BLK = 64
WID = 384
HID = 1536
HALF = 768
NCH = 4
CHR = 256
RZ = CHR // NZ
SUM_SCALE = 2.0**19
OUT_SCALE = 2.0**9

STEPS = [0, 1, 3, 2]
PART = CHR // 2
SUB = BLK // 2
BLOCKWISE = (2, 3)


def gelu_exact(values):
    return values * 0.5 * (1.0 + lax.erf(values * 0.7071067811865476))


def gelu_slope(values):
    normal_cdf = 0.5 * (1.0 + lax.erf(values * 0.7071067811865476))
    return normal_cdf + values * jnp.exp(-0.5 * values * values) * 0.3989422804014327


def enc(v):
    return ((v * jnp.abs(v)) * (v * v)).astype(BF16)


def dec(code):
    y = code.astype(F32)
    root = lax.rsqrt(lax.rsqrt(jnp.abs(y)))
    return jnp.where(y == 0.0, 0.0, jnp.where(y < 0.0, -root, root))


def kernel(
    tok_ref, win_hbm, wout_hbm, dout_ref,
    out_ref, gt_ref, gwi_ref, gwo_ref,
    win_ref, wout_ref, acts, xs, wc0, wc1, part, snd, rcv, hid, osnd, orcv, osum,
    loc_sem, one_s, one_r, two_s, two_r, fwd_s, fwd_r, w_s, w_r,
    rs_s, rs_r, ag_s, ag_r, sib_s, sib_r, blk_s, blk_r, out_s, out_r,
):
    row = lax.axis_index("row")
    col = lax.axis_index("col")
    z, core = row // 2, row % 2
    x, y = col // 4, col % 4
    other = 1 - core
    sib = (z * 2 + other, col)
    z_to = [(((z + 1) % NZ) * 2 + core, col), (((z + NZ - 1) % NZ) * 2 + core, col)]

    def shift(by):
        return (z + by + NZ) % NZ

    def peer(dx, dy):
        return (row, ((x + dx + 4) % 4) * 4 + (y + dy + 4) % 4)

    own_w = pl.ds(pl.multiple_of(core * WID, WID), WID)
    own_h = pl.ds(pl.multiple_of(core * HALF, HALF), HALF)
    oth_h = pl.ds(pl.multiple_of(other * HALF, HALF), HALF)
    halves = [pl.ds(0, WID), pl.ds(WID, WID)]
    x_in = [tok_ref, dout_ref]

    def remote(src, dst, s, r, dev):
        return pltpu.make_async_remote_copy(
            src_ref=src, dst_ref=dst, send_sem=s, recv_sem=r, device_id=dev, device_id_type=MESH
        )

    barrier = pltpu.get_barrier_semaphore()
    greeted = [sib, *z_to] + [peer(dx, dy) for dx in range(4) for dy in range(4) if dx or dy]
    for dev in greeted:
        pl.semaphore_signal(barrier, inc=1, device_id=dev, device_id_type=MESH)
    local = [
        pltpu.make_async_copy(
            x_in[t].at[pl.ds(ab * SUB, SUB), :], xs.at[t, pl.ds(ab * PART, SUB), own_w], loc_sem.at[t * 2 + ab]
        )
        for t in range(2)
        for ab in range(2)
    ]
    local += [
        pltpu.make_async_copy(win_hbm.at[:, own_h], wc0.at[own_w, :], loc_sem.at[4]),
        pltpu.make_async_copy(wout_hbm.at[own_h, :], wc1.at[:, own_w], loc_sem.at[5]),
        pltpu.make_async_copy(win_hbm, win_ref, loc_sem.at[6]),
        pltpu.make_async_copy(wout_hbm, wout_ref, loc_sem.at[7]),
    ]
    for c in local:
        c.start()
    pl.semaphore_wait(barrier, len(greeted))

    def one_copy(t, ab, i):
        to = peer(0, -STEPS[i]) if ab == 0 else peer(-STEPS[i], 0)
        return remote(
            x_in[t].at[pl.ds(ab * SUB, SUB), :],
            xs.at[t, pl.ds(ab * PART + i * SUB, SUB), own_w],
            one_s.at[t, ab, i], one_r.at[t, ab, i], to,
        )

    def two_copy(t, ab, j):
        to = peer(-STEPS[j], 0) if ab == 0 else peer(0, -STEPS[j])
        return remote(
            xs.at[t, pl.ds(ab * PART, PART), own_w],
            xs.at[t, pl.ds(j * CHR + ab * PART, PART), own_w],
            two_s.at[t, ab, j], two_r.at[t, ab, j], to,
        )

    def fwd_copy(t, k):
        place = xs.at[t, pl.ds(k * CHR, CHR), own_w]
        return remote(place, place, fwd_s.at[t, k], fwd_r.at[t, k], sib)

    w_copies = [
        remote(win_hbm.at[:, oth_h], wc0.at[own_w, :], w_s.at[0], w_r.at[0], sib),
        remote(wout_hbm.at[oth_h, :], wc1.at[:, own_w], w_s.at[1], w_r.at[1], sib),
    ]

    def spread(t, j):
        for ab in range(2):
            two_copy(t, ab, j).start()

    def arrive(t, k):
        for ab in range(2):
            if k:
                two_copy(t, ab, k).wait_recv()
            else:
                local[t * 2 + ab].wait()
                for i in range(1, 4):
                    one_copy(t, ab, i).wait_recv()
        fwd_copy(t, k).start()

    def partial(t, k):
        fwd_copy(t, k).wait_recv()
        rows = pl.ds(k * CHR, CHR)

        if t == 0:
            got = jnp.dot(xs[0, rows, :], wc0[...], preferred_element_type=F32)
        else:
            got = lax.dot_general(xs[1, rows, :], wc1[...], (((1,), (1,)), ((), ())), preferred_element_type=F32)
        part[t, k] = got * SUM_SCALE

    def rs_copy(t, k, d, r):
        at = (t, k, d, r)
        if r == 0:
            src, dst = snd.at[t, k, d, r, :, halves[d]], rcv.at[t, k, d, r, :, halves[d]]
        else:
            src, dst = snd.at[at], rcv.at[at]
        return remote(src, dst, rs_s.at[at], rs_r.at[at], z_to[d])

    def rs_one(t, k, r):
        for d in range(2):
            owner = shift(4 - r if d == 0 else r - 4)
            rows = pl.ds(pl.multiple_of(owner * RZ, RZ), RZ)
            mine = halves[d]
            if r == 0:
                snd[t, k, d, r, :, mine] = enc(part[t, k, rows, mine])
            else:
                rs_copy(t, k, d, r - 1).wait_recv()
                if r == 1:
                    rest = halves[1 - d]
                    snd[t, k, d, r, :, mine] = enc(dec(rcv[t, k, d, 0, :, mine]) + part[t, k, rows, mine])
                    snd[t, k, d, r, :, rest] = enc(part[t, k, rows, rest])
                else:
                    snd[t, k, d, r] = enc(dec(rcv[t, k, d, r - 1]) + part[t, k, rows, :])
            rs_copy(t, k, d, r).start()

    def both(fn):
        def body(t, carry):
            fn(t)
            return carry

        lax.fori_loop(0, 2, body, 0)

    def rs(k, r):
        both(lambda t: rs_one(t, k, r))

    def ag_copy(t, k, d, r, b):
        rows = pl.ds(pl.multiple_of(k * CHR + b * RZ, RZ), RZ)
        if r == 3:
            cols = pl.ds(pl.multiple_of(core * HALF + d * WID, WID), WID)
        else:
            cols = own_h
        place = acts.at[t, rows, cols]
        return remote(place, place, ag_s.at[t, k, d, r], ag_r.at[t, k, d, r], z_to[d])

    def ag_wait(t, k, d, r):
        ag_copy(t, k, d, r, shift(-(r + 1) if d == 0 else r + 1)).wait_recv()

    def ag_one(t, k, r):
        for d in range(2):
            if r:
                ag_wait(t, k, d, r - 1)
            block = shift(-r if d == 0 else r)
            ag_copy(t, k, d, r, block).start()
            if k in BLOCKWISE and (r or d == 0):
                blk_copy(t, k, d * 3 + r, block).start()

    def ag(k, r):
        both(lambda t: ag_one(t, k, r))

    def settle(k):
        rows = pl.ds(pl.multiple_of(z * RZ, RZ), RZ)
        place = pl.ds(pl.multiple_of(k * CHR + z * RZ, RZ), RZ)
        for t in range(2):
            for d in range(2):
                rs_copy(t, k, d, 3).wait_recv()
            total = (dec(rcv[t, k, 0, 3]) + dec(rcv[t, k, 1, 3]) + part[t, k, rows, :]) * (1.0 / SUM_SCALE)
            if t == 0:
                hid[...] = total
                acts[0, place, own_h] = gelu_exact(total).astype(BF16)
            else:
                acts[1, place, own_h] = (total * gelu_slope(hid[...])).astype(BF16)
            ag_one(t, k, 0)

    def sib_copy(t, k):
        place = acts.at[t, pl.ds(k * CHR, CHR), own_h]
        return remote(place, place, sib_s.at[t, k], sib_r.at[t, k], sib)

    def blk_copy(t, k, i, block):
        rows = pl.ds(pl.multiple_of(k * CHR + block * RZ, RZ), RZ)
        place = acts.at[t, rows, own_h]
        at = (t, k - BLOCKWISE[0], i)
        return remote(place, place, blk_s.at[at], blk_r.at[at], sib)

    def block_at(i):
        return shift(-i if i < 4 else i - 3) if i < 7 else shift(4)

    def gathered(k):
        for t in range(2):
            for d in range(2):
                ag_wait(t, k, d, 3)
            if k in BLOCKWISE:
                blk_copy(t, k, 7, shift(4)).start()
            else:
                sib_copy(t, k).start()

    def out_copy(t, ab, n):
        near, far = STEPS[n // 4], STEPS[n % 4]
        to = peer(near, far) if ab == 0 else peer(far, near)
        return remote(osnd.at[t, ab, n], orcv.at[t, ab, n], out_s.at[t, ab, n], out_r.at[t, ab, n], to)

    def project(k, ts=(0, 1)):
        rows = pl.ds(k * CHR, CHR)
        for t in ts:
            if k in BLOCKWISE:
                for i in range(8):
                    blk_copy(t, k, i, block_at(i)).wait_recv()
            else:
                sib_copy(t, k).wait_recv()
            if t == 0:
                got = jnp.dot(acts[0, rows, :], wout_ref[...], preferred_element_type=F32)
            else:
                got = lax.dot_general(
                    acts[1, rows, :], win_ref[...], (((1,), (1,)), ((), ())), preferred_element_type=F32
                )
            got = got * OUT_SCALE
            for ab in range(2):
                for i in range(4):
                    n = 4 * k + i
                    block = got[ab * PART + i * SUB : ab * PART + (i + 1) * SUB, :]
                    if n == 0:
                        osum[t, pl.ds(ab * SUB, SUB), :] = block
                    else:
                        osnd[t, ab, n] = enc(block)
                        out_copy(t, ab, n).start()

    def grad_w_out(k):
        rows = pl.ds(k * CHR, 2 * CHR)

        def tile(n, carry):
            cols = pl.ds(pl.multiple_of(n * 256, 256), 256)
            more = lax.dot_general(
                acts[0, rows, cols], xs[1, rows, own_w], (((0,), (0,)), ((), ())), preferred_element_type=F32
            )
            gwo_ref[cols, :] = more if k == 0 else gwo_ref[cols, :] + more
            return carry

        lax.fori_loop(0, HID // 256, tile, 0)

    def grad_w_in(k):
        rows = pl.ds(k * CHR, 2 * CHR)

        def tile(n, carry):
            cols = pl.ds(pl.multiple_of(n * 256, 256), 256)
            more = lax.dot_general(
                xs[0, rows, own_w], acts[1, rows, cols], (((0,), (0,)), ((), ())), preferred_element_type=F32
            )
            gwi_ref[:, cols] = more if k == 0 else gwi_ref[:, cols] + more
            return carry

        lax.fori_loop(0, HID // 256, tile, 0)

    for t in range(2):
        for i in range(1, 4):
            for ab in range(2):
                one_copy(t, ab, i).start()
        w_copies[t].start()
    for t in range(2):
        arrive(t, 0)
        spread(t, 1)
        spread(t, 2)
    for t in range(2):
        local[4 + t].wait()
        w_copies[t].wait_recv()
        partial(t, 0)
        rs_one(t, 0, 0)
    for t in range(2):
        arrive(t, 1)
        rs_one(t, 0, 1)
    for t in range(2):
        partial(t, 1)
        rs_one(t, 1, 0)
    for t in range(2):
        arrive(t, 2)
        spread(t, 3)
    rs(0, 2)
    for t in range(2):
        partial(t, 2)
        rs_one(t, 2, 0)
    rs(1, 1)
    rs(0, 3); rs(1, 2); rs(2, 1)
    for t in range(2):
        arrive(t, 3)
    settle(0); rs(1, 3); rs(2, 2)
    for t in range(2):
        partial(t, 3)
        rs_one(t, 3, 0)
    ag(0, 1); settle(1); rs(2, 3); rs(3, 1)
    ag(0, 2); ag(1, 1); settle(2); rs(3, 2)
    ag(0, 3); ag(1, 2); ag(2, 1); rs(3, 3)
    for t in range(2):
        local[6 + t].wait()
    gathered(0); ag(1, 3); ag(2, 2); settle(3)
    project(0)
    gathered(1); ag(2, 3); ag(3, 1)
    project(1, (0,))
    gathered(2); ag(3, 2)
    project(1, (1,))
    project(2, (0,))
    ag(3, 3)
    project(2, (1,))
    gathered(3)
    project(3)
    grad_w_out(0)
    grad_w_in(0)
    grad_w_out(2)
    grad_w_in(2)
    for t in range(2):
        for ab in range(2):
            rows = pl.ds(ab * SUB, SUB)

            def add(n, carry, t=t, ab=ab, rows=rows):
                remote(
                    osnd.at[t, ab, n], orcv.at[t, ab, n], out_s.at[t, ab, n], out_r.at[t, ab, n], sib
                ).wait_recv()
                osum[t, rows, :] = osum[t, rows, :] + dec(orcv[t, ab, n])
                return carry

            lax.fori_loop(1, 16, add, 0)
    out_ref[...] = osum[0] * (1.0 / OUT_SCALE)
    gt_ref[...] = osum[1] * (1.0 / OUT_SCALE)

    for t in range(2):
        w_copies[t].wait_send()
        for ab in range(2):
            for i in range(1, 4):
                one_copy(t, ab, i).wait_send()
                two_copy(t, ab, i).wait_send()
            for n in range(1, 16):
                out_copy(t, ab, n).wait_send()
        for k in range(NCH):
            fwd_copy(t, k).wait_send()
            if k in BLOCKWISE:
                for i in range(8):
                    blk_copy(t, k, i, block_at(i)).wait_send()
            else:
                sib_copy(t, k).wait_send()
            for d in range(2):
                for r in range(4):
                    rs_copy(t, k, d, r).wait_send()
                    ag_copy(t, k, d, r, shift(-r if d == 0 else r)).wait_send()


def store(out_v, gt_v, gwi_v, gwo_v, out_ref, gt_ref, gwi_ref, gwo_ref, sems):
    pairs = [(gwi_v, gwi_ref), (gwo_v, gwo_ref), (out_v, out_ref), (gt_v, gt_ref)]
    copies = [pltpu.make_async_copy(a, b, sems.at[i]) for i, (a, b) in enumerate(pairs)]
    for c in copies:
        c.start()
    for c in copies:
        c.wait()


def shards(tokens, w_in, w_out, d_output):
    vmem = pl.BlockSpec(memory_space=pltpu.VMEM)
    dma = pltpu.SemaphoreType.DMA
    shapes = [(BLK, WID), (BLK, WID), (WID, HID), (HID, WID)]
    results = pl.pallas_call(
        kernel,
        out_shape=tuple(pltpu.VMEM(shape, F32) for shape in shapes),
        in_specs=[pl.BlockSpec(memory_space=pl.ANY)] * 4,
        out_specs=(vmem,) * 4,
        scratch_shapes=[
            pltpu.VMEM((WID, HID), BF16),
            pltpu.VMEM((HID, WID), BF16),
            pltpu.VMEM((2, NCH * CHR, HID), BF16),
            pltpu.VMEM((2, NCH * CHR, HALF), BF16),
            pltpu.VMEM((HALF, HALF), BF16),
            pltpu.VMEM((HALF, HALF), BF16),
            pltpu.VMEM((2, NCH, CHR, HALF), F32),
            pltpu.VMEM((2, NCH, 2, 4, RZ, HALF), BF16),
            pltpu.VMEM((2, NCH, 2, 4, RZ, HALF), BF16),
            pltpu.VMEM((RZ, HALF), F32),
            pltpu.VMEM((2, 2, 16, SUB, WID), BF16),
            pltpu.VMEM((2, 2, 16, SUB, WID), BF16),
            pltpu.VMEM((2, BLK, WID), F32),
            dma((8,)),
            dma((2, 2, 4)), dma((2, 2, 4)),
            dma((2, 2, 4)), dma((2, 2, 4)),
            dma((2, NCH)), dma((2, NCH)),
            dma((2,)), dma((2,)),
            dma((2, NCH, 2, 4)), dma((2, NCH, 2, 4)),
            dma((2, NCH, 2, 4)), dma((2, NCH, 2, 4)),
            dma((2, NCH)), dma((2, NCH)),
            dma((2, 2, 8)), dma((2, 2, 8)),
            dma((2, 2, 16)), dma((2, 2, 16)),
        ],
        compiler_params=pltpu.CompilerParams(
            collective_id=0, has_side_effects=True, vmem_limit_bytes=56 * 2**20
        ),
    )(tokens, w_in, w_out, d_output)
    return pl.pallas_call(
        store,
        out_shape=tuple(jax.ShapeDtypeStruct(shape, F32) for shape in shapes),
        in_specs=[pl.BlockSpec(memory_space=pl.ANY)] * 4,
        out_specs=(pl.BlockSpec(memory_space=pl.ANY),) * 4,
        scratch_shapes=[dma((4,))],
        compiler_params=pltpu.CompilerParams(vmem_limit_bytes=2**20),
    )(*results)


def solution(mesh):
    placed = (P("col", "row"), P("row", "col"), P("col", "row"), P("col", "row"))
    return jax.shard_map(
        shards,
        mesh=mesh,
        in_specs=placed,
        out_specs=(P("col", "row"), P("col", "row"), P("row", "col"), P("col", "row")),
        check_vma=False,
    )
```

```python
import functools

import jax
import jax.numpy as jnp
from jax import lax
from jax.experimental import pallas as pl
from jax.experimental.pallas import tpu as pltpu
from jax.sharding import PartitionSpec as P

F32, BF16 = jnp.float32, jnp.bfloat16
MESH = pl.DeviceIdType.MESH
NZ = 8
BLK = 64
WID = 384
HID = 1536
HALF = 768
NCH = 4
CHR = 256
RZ = CHR // NZ
SUM_SCALE = 2.0**19
OUT_SCALE = 2.0**9

STEPS = [0, 1, 3, 2]
PART = CHR // 2
SUB = BLK // 2
BLOCKWISE = (2, 3)


def gelu_exact(values):
    return values * 0.5 * (1.0 + lax.erf(values * 0.7071067811865476))


def gelu_slope(values):
    normal_cdf = 0.5 * (1.0 + lax.erf(values * 0.7071067811865476))
    return normal_cdf + values * jnp.exp(-0.5 * values * values) * 0.3989422804014327


def enc(v):
    return ((v * jnp.abs(v)) * (v * v)).astype(BF16)


def dec(code):
    y = code.astype(F32)
    root = lax.rsqrt(lax.rsqrt(jnp.abs(y)))
    return jnp.where(y == 0.0, 0.0, jnp.where(y < 0.0, -root, root))


def kernel(
    tok_ref, win_hbm, wout_hbm, dout_ref,
    out_ref, gt_ref, gwi_ref, gwo_ref,
    win_ref, wout_ref, acts, xs, wc0, wc1, part, snd, rcv, hid, osnd, orcv, osum,
    loc_sem, one_s, one_r, two_s, two_r, fwd_s, fwd_r, w_s, w_r,
    rs_s, rs_r, ag_s, ag_r, sib_s, sib_r, blk_s, blk_r, out_s, out_r,
):
    row = lax.axis_index("row")
    col = lax.axis_index("col")
    z, core = row // 2, row % 2
    x, y = col // 4, col % 4
    other = 1 - core
    sib = (z * 2 + other, col)
    z_to = [(((z + 1) % NZ) * 2 + core, col), (((z + NZ - 1) % NZ) * 2 + core, col)]

    def shift(by):
        return (z + by + NZ) % NZ

    def peer(dx, dy):
        return (row, ((x + dx + 4) % 4) * 4 + (y + dy + 4) % 4)

    own_w = pl.ds(pl.multiple_of(core * WID, WID), WID)
    own_h = pl.ds(pl.multiple_of(core * HALF, HALF), HALF)
    oth_h = pl.ds(pl.multiple_of(other * HALF, HALF), HALF)
    halves = [pl.ds(0, WID), pl.ds(WID, WID)]
    x_in = [tok_ref, dout_ref]

    def remote(src, dst, s, r, dev):
        return pltpu.make_async_remote_copy(
            src_ref=src, dst_ref=dst, send_sem=s, recv_sem=r, device_id=dev, device_id_type=MESH
        )

    barrier = pltpu.get_barrier_semaphore()
    greeted = [sib, *z_to] + [peer(dx, dy) for dx in range(4) for dy in range(4) if dx or dy]
    for dev in greeted:
        pl.semaphore_signal(barrier, inc=1, device_id=dev, device_id_type=MESH)
    local = [
        pltpu.make_async_copy(
            x_in[t].at[pl.ds(ab * SUB, SUB), :], xs.at[t, pl.ds(ab * PART, SUB), own_w], loc_sem.at[t * 2 + ab]
        )
        for t in range(2)
        for ab in range(2)
    ]
    local += [
        pltpu.make_async_copy(win_hbm.at[:, own_h], wc0.at[own_w, :], loc_sem.at[4]),
        pltpu.make_async_copy(wout_hbm.at[own_h, :], wc1.at[:, own_w], loc_sem.at[5]),
        pltpu.make_async_copy(win_hbm, win_ref, loc_sem.at[6]),
        pltpu.make_async_copy(wout_hbm, wout_ref, loc_sem.at[7]),
    ]
    for c in local:
        c.start()
    pl.semaphore_wait(barrier, len(greeted))

    def one_copy(t, ab, i):
        to = peer(0, -STEPS[i]) if ab == 0 else peer(-STEPS[i], 0)
        return remote(
            x_in[t].at[pl.ds(ab * SUB, SUB), :],
            xs.at[t, pl.ds(ab * PART + i * SUB, SUB), own_w],
            one_s.at[t, ab, i], one_r.at[t, ab, i], to,
        )

    def two_copy(t, ab, j):
        to = peer(-STEPS[j], 0) if ab == 0 else peer(0, -STEPS[j])
        return remote(
            xs.at[t, pl.ds(ab * PART, PART), own_w],
            xs.at[t, pl.ds(j * CHR + ab * PART, PART), own_w],
            two_s.at[t, ab, j], two_r.at[t, ab, j], to,
        )

    def fwd_copy(t, k, ab):
        place = xs.at[t, pl.ds(k * CHR + ab * PART, PART), own_w]
        return remote(place, place, fwd_s.at[t, k, ab], fwd_r.at[t, k, ab], sib)

    w_copies = [
        remote(win_hbm.at[:, oth_h], wc0.at[own_w, :], w_s.at[0], w_r.at[0], sib),
        remote(wout_hbm.at[oth_h, :], wc1.at[:, own_w], w_s.at[1], w_r.at[1], sib),
    ]

    def spread(t, j):
        for ab in range(2):
            two_copy(t, ab, j).start()

    def arrive(t, k):
        for ab in range(2):
            if k:
                two_copy(t, ab, k).wait_recv()
            else:
                local[t * 2 + ab].wait()
                for i in range(1, 4):
                    one_copy(t, ab, i).wait_recv()
            fwd_copy(t, k, ab).start()

    def partial(t, k):
        for ab in range(2):
            fwd_copy(t, k, ab).wait_recv()
        rows = pl.ds(k * CHR, CHR)

        if t == 0:
            got = jnp.dot(xs[0, rows, :], wc0[...], preferred_element_type=F32)
        else:
            got = lax.dot_general(xs[1, rows, :], wc1[...], (((1,), (1,)), ((), ())), preferred_element_type=F32)
        part[t, k] = got * SUM_SCALE

    def rs_copy(t, k, d, r):
        at = (t, k, d, r)
        if r == 0:
            src, dst = snd.at[t, k, d, r, :, halves[d]], rcv.at[t, k, d, r, :, halves[d]]
        else:
            src, dst = snd.at[at], rcv.at[at]
        return remote(src, dst, rs_s.at[at], rs_r.at[at], z_to[d])

    def rs_one(t, k, r):
        for d in range(2):
            owner = shift(4 - r if d == 0 else r - 4)
            rows = pl.ds(pl.multiple_of(owner * RZ, RZ), RZ)
            mine = halves[d]
            if r == 0:
                snd[t, k, d, r, :, mine] = enc(part[t, k, rows, mine])
            else:
                rs_copy(t, k, d, r - 1).wait_recv()
                if r == 1:
                    rest = halves[1 - d]
                    snd[t, k, d, r, :, mine] = enc(dec(rcv[t, k, d, 0, :, mine]) + part[t, k, rows, mine])
                    snd[t, k, d, r, :, rest] = enc(part[t, k, rows, rest])
                else:
                    snd[t, k, d, r] = enc(dec(rcv[t, k, d, r - 1]) + part[t, k, rows, :])
            rs_copy(t, k, d, r).start()

    def both(fn):
        def body(t, carry):
            fn(t)
            return carry

        lax.fori_loop(0, 2, body, 0)

    def rs(k, r):
        both(lambda t: rs_one(t, k, r))

    def ag_copy(t, k, d, r, b):
        rows = pl.ds(pl.multiple_of(k * CHR + b * RZ, RZ), RZ)
        if r == 3:
            cols = pl.ds(pl.multiple_of(core * HALF + d * WID, WID), WID)
        else:
            cols = own_h
        place = acts.at[t, rows, cols]
        return remote(place, place, ag_s.at[t, k, d, r], ag_r.at[t, k, d, r], z_to[d])

    def ag_wait(t, k, d, r):
        ag_copy(t, k, d, r, shift(-(r + 1) if d == 0 else r + 1)).wait_recv()

    def ag_one(t, k, r):
        for d in range(2):
            if r:
                ag_wait(t, k, d, r - 1)
            block = shift(-r if d == 0 else r)
            ag_copy(t, k, d, r, block).start()
            if k in BLOCKWISE and (r or d == 0):
                blk_copy(t, k, d * 3 + r, block).start()

    def ag(k, r):
        both(lambda t: ag_one(t, k, r))

    def settle(k):
        rows = pl.ds(pl.multiple_of(z * RZ, RZ), RZ)
        place = pl.ds(pl.multiple_of(k * CHR + z * RZ, RZ), RZ)
        for t in range(2):
            for d in range(2):
                rs_copy(t, k, d, 3).wait_recv()
            total = (dec(rcv[t, k, 0, 3]) + dec(rcv[t, k, 1, 3]) + part[t, k, rows, :]) * (1.0 / SUM_SCALE)
            if t == 0:
                hid[...] = total
                acts[0, place, own_h] = gelu_exact(total).astype(BF16)
            else:
                acts[1, place, own_h] = (total * gelu_slope(hid[...])).astype(BF16)
            ag_one(t, k, 0)

    def sib_copy(t, k):
        place = acts.at[t, pl.ds(k * CHR, CHR), own_h]
        return remote(place, place, sib_s.at[t, k], sib_r.at[t, k], sib)

    def blk_copy(t, k, i, block):
        rows = pl.ds(pl.multiple_of(k * CHR + block * RZ, RZ), RZ)
        place = acts.at[t, rows, own_h]
        at = (t, k - BLOCKWISE[0], i)
        return remote(place, place, blk_s.at[at], blk_r.at[at], sib)

    def block_at(i):
        return shift(-i if i < 4 else i - 3) if i < 7 else shift(4)

    def gathered(k):
        for t in range(2):
            for d in range(2):
                ag_wait(t, k, d, 3)
            if k in BLOCKWISE:
                blk_copy(t, k, 7, shift(4)).start()
            else:
                sib_copy(t, k).start()

    def out_copy(t, ab, n):
        near, far = STEPS[n // 4], STEPS[n % 4]
        to = peer(near, far) if ab == 0 else peer(far, near)
        return remote(osnd.at[t, ab, n], orcv.at[t, ab, n], out_s.at[t, ab, n], out_r.at[t, ab, n], to)

    def project(k, ts=(0, 1)):
        rows = pl.ds(k * CHR, CHR)

        def product(t, cols):
            if t == 0:
                return jnp.dot(acts[0, rows, cols], wout_ref[cols, :], preferred_element_type=F32)
            return lax.dot_general(
                acts[1, rows, cols], win_ref[:, cols], (((1,), (1,)), ((), ())), preferred_element_type=F32
            )

        first = [product(t, own_h) for t in ts]
        for t, got in zip(ts, first):
            if k in BLOCKWISE:
                for i in range(8):
                    blk_copy(t, k, i, block_at(i)).wait_recv()
            else:
                sib_copy(t, k).wait_recv()
            got = got + product(t, oth_h)
            got = got * OUT_SCALE
            for ab in range(2):
                for i in range(4):
                    n = 4 * k + i
                    block = got[ab * PART + i * SUB : ab * PART + (i + 1) * SUB, :]
                    if n == 0:
                        osum[t, pl.ds(ab * SUB, SUB), :] = block
                    else:
                        osnd[t, ab, n] = enc(block)
                        out_copy(t, ab, n).start()

    def grad_w_out(k):
        rows = pl.ds(k * CHR, 2 * CHR)

        def tile(n, carry):
            cols = pl.ds(pl.multiple_of(n * 256, 256), 256)
            more = lax.dot_general(
                acts[0, rows, cols], xs[1, rows, own_w], (((0,), (0,)), ((), ())), preferred_element_type=F32
            )
            gwo_ref[cols, :] = more if k == 0 else gwo_ref[cols, :] + more
            return carry

        lax.fori_loop(0, HID // 256, tile, 0)

    def grad_w_in(k):
        rows = pl.ds(k * CHR, 2 * CHR)

        def tile(n, carry):
            cols = pl.ds(pl.multiple_of(n * 256, 256), 256)
            more = lax.dot_general(
                xs[0, rows, own_w], acts[1, rows, cols], (((0,), (0,)), ((), ())), preferred_element_type=F32
            )
            gwi_ref[:, cols] = more if k == 0 else gwi_ref[:, cols] + more
            return carry

        lax.fori_loop(0, HID // 256, tile, 0)

    for t in range(2):
        for i in range(1, 4):
            for ab in range(2):
                one_copy(t, ab, i).start()
        w_copies[t].start()
    for t in range(2):
        arrive(t, 0)
        spread(t, 1)
        spread(t, 2)
    for t in range(2):
        local[4 + t].wait()
        w_copies[t].wait_recv()
        partial(t, 0)
        rs_one(t, 0, 0)
    for t in range(2):
        arrive(t, 1)
        rs_one(t, 0, 1)
    for t in range(2):
        partial(t, 1)
        rs_one(t, 1, 0)
    for t in range(2):
        arrive(t, 2)
        spread(t, 3)
    rs(0, 2)
    for t in range(2):
        partial(t, 2)
        rs_one(t, 2, 0)
    rs(1, 1)
    rs(0, 3); rs(1, 2); rs(2, 1)
    for t in range(2):
        arrive(t, 3)
    settle(0); rs(1, 3); rs(2, 2)
    for t in range(2):
        partial(t, 3)
        rs_one(t, 3, 0)
    ag(0, 1); settle(1); rs(2, 3); rs(3, 1)
    ag(0, 2); ag(1, 1); settle(2); rs(3, 2)
    ag(0, 3); ag(1, 2); ag(2, 1); rs(3, 3)
    for t in range(2):
        local[6 + t].wait()
    gathered(0); ag(1, 3); ag(2, 2); settle(3)
    project(0)
    gathered(1); ag(2, 3); ag(3, 1)
    project(1, (0,))
    gathered(2); ag(3, 2)
    project(1, (1,))
    project(2, (0,))
    ag(3, 3)
    project(2, (1,))
    gathered(3)
    project(3)
    grad_w_out(0)
    grad_w_in(0)
    grad_w_out(2)
    grad_w_in(2)
    for t in range(2):
        for ab in range(2):
            rows = pl.ds(ab * SUB, SUB)

            def add(n, carry, t=t, ab=ab, rows=rows):
                remote(
                    osnd.at[t, ab, n], orcv.at[t, ab, n], out_s.at[t, ab, n], out_r.at[t, ab, n], sib
                ).wait_recv()
                osum[t, rows, :] = osum[t, rows, :] + dec(orcv[t, ab, n])
                return carry

            lax.fori_loop(1, 16, add, 0)
    out_ref[...] = osum[0] * (1.0 / OUT_SCALE)
    gt_ref[...] = osum[1] * (1.0 / OUT_SCALE)

    for t in range(2):
        w_copies[t].wait_send()
        for ab in range(2):
            for i in range(1, 4):
                one_copy(t, ab, i).wait_send()
                two_copy(t, ab, i).wait_send()
            for n in range(1, 16):
                out_copy(t, ab, n).wait_send()
        for k in range(NCH):
            for ab in range(2):
                fwd_copy(t, k, ab).wait_send()
            if k in BLOCKWISE:
                for i in range(8):
                    blk_copy(t, k, i, block_at(i)).wait_send()
            else:
                sib_copy(t, k).wait_send()
            for d in range(2):
                for r in range(4):
                    rs_copy(t, k, d, r).wait_send()
                    ag_copy(t, k, d, r, shift(-r if d == 0 else r)).wait_send()


def store(out_v, gt_v, gwi_v, gwo_v, out_ref, gt_ref, gwi_ref, gwo_ref, sems):
    pairs = [(gwi_v, gwi_ref), (gwo_v, gwo_ref), (out_v, out_ref), (gt_v, gt_ref)]
    copies = [pltpu.make_async_copy(a, b, sems.at[i]) for i, (a, b) in enumerate(pairs)]
    for c in copies:
        c.start()
    for c in copies:
        c.wait()


def shards(tokens, w_in, w_out, d_output):
    vmem = pl.BlockSpec(memory_space=pltpu.VMEM)
    dma = pltpu.SemaphoreType.DMA
    shapes = [(BLK, WID), (BLK, WID), (WID, HID), (HID, WID)]
    results = pl.pallas_call(
        kernel,
        out_shape=tuple(pltpu.VMEM(shape, F32) for shape in shapes),
        in_specs=[pl.BlockSpec(memory_space=pl.ANY)] * 4,
        out_specs=(vmem,) * 4,
        scratch_shapes=[
            pltpu.VMEM((WID, HID), BF16),
            pltpu.VMEM((HID, WID), BF16),
            pltpu.VMEM((2, NCH * CHR, HID), BF16),
            pltpu.VMEM((2, NCH * CHR, HALF), BF16),
            pltpu.VMEM((HALF, HALF), BF16),
            pltpu.VMEM((HALF, HALF), BF16),
            pltpu.VMEM((2, NCH, CHR, HALF), F32),
            pltpu.VMEM((2, NCH, 2, 4, RZ, HALF), BF16),
            pltpu.VMEM((2, NCH, 2, 4, RZ, HALF), BF16),
            pltpu.VMEM((RZ, HALF), F32),
            pltpu.VMEM((2, 2, 16, SUB, WID), BF16),
            pltpu.VMEM((2, 2, 16, SUB, WID), BF16),
            pltpu.VMEM((2, BLK, WID), F32),
            dma((8,)),
            dma((2, 2, 4)), dma((2, 2, 4)),
            dma((2, 2, 4)), dma((2, 2, 4)),
            dma((2, NCH, 2)), dma((2, NCH, 2)),
            dma((2,)), dma((2,)),
            dma((2, NCH, 2, 4)), dma((2, NCH, 2, 4)),
            dma((2, NCH, 2, 4)), dma((2, NCH, 2, 4)),
            dma((2, NCH)), dma((2, NCH)),
            dma((2, 2, 8)), dma((2, 2, 8)),
            dma((2, 2, 16)), dma((2, 2, 16)),
        ],
        compiler_params=pltpu.CompilerParams(
            collective_id=0, has_side_effects=True, vmem_limit_bytes=56 * 2**20
        ),
    )(tokens, w_in, w_out, d_output)
    return pl.pallas_call(
        store,
        out_shape=tuple(jax.ShapeDtypeStruct(shape, F32) for shape in shapes),
        in_specs=[pl.BlockSpec(memory_space=pl.ANY)] * 4,
        out_specs=(pl.BlockSpec(memory_space=pl.ANY),) * 4,
        scratch_shapes=[dma((4,))],
        compiler_params=pltpu.CompilerParams(vmem_limit_bytes=2**20),
    )(*results)


def solution(mesh):
    placed = (P("col", "row"), P("row", "col"), P("col", "row"), P("col", "row"))
    return jax.shard_map(
        shards,
        mesh=mesh,
        in_specs=placed,
        out_specs=(P("col", "row"), P("col", "row"), P("row", "col"), P("col", "row")),
        check_vma=False,
    )
```
